32 devices in a mesh: rows: 8 (over z, x), tm: 4 (over y, core).
Axes of the slice: x: 2, y: 2, z: 4, core: 2. Of those that a mesh axis runs over, the one named last changes fastest.
Arguments:
- counts: int32 [8192, 2048], P('rows', 'tm'), may hold values from 0 to 3
- col_blocks: int32 [64, 24], P('rows'), may hold values from 0 to 63, as said below
- kernel: bfloat16 [64, 24, 128, 128], P('rows'), may hold values from -0.109375 to 0.109375
- mixing: float32 [8, 8192], P(None, 'rows'), may hold values from -6.3 to 6.3
- decay_rate: float32 [8], replicated, may hold values from 0.0001 to 0.04
- baseline: float32 [8192], P('rows'), may hold values from -6 to 6
Outputs:
- intensity: bfloat16 [8192, 2048], P('rows', 'tm')
The draws below stay inside these ranges and needn't reach their ends.
Inputs may be any that keep to these rules, and one draw needn't show every extreme that they name: The 24 entries of a block row are different blocks, and each lies within two indices of rows of the row's own on either side, cyclically: (col_blocks[I, k] // 8 - I // 8) mod 8 is 0, 1, 2, 8 - 1 or 8 - 2.
All inputs are finite; a program needn't handle non-finite values.
Results may differ from the reference program's by a relative error of at most 0.0034.
Values may be sent and summed in bfloat16 or wider, within the bound.
A program may use at most 128 MiB of HBM per device.

```python
import jax
import jax.numpy as jnp
from jax import lax

BLK = 128
BASES = 8
SLOTS = 24
BR_DEV = 8
NB = 64
TYPES = 8192
TIME = 2048


def basis_roles(key):
    return jax.random.permutation(jax.random.fold_in(key, 101), BASES).astype(jnp.int32)


def draw_col_blocks(key, part):
    row_ids = jnp.arange(NB, dtype=jnp.int32)
    device = row_ids // BR_DEV
    window_len = 5 * BR_DEV
    scores = jax.random.randint(key, (NB, window_len), 0, 1 << 20) * window_len + jnp.arange(window_len, dtype=jnp.int32)[None, :]
    chosen = jnp.argsort(scores, axis=1)[:, :SLOTS].astype(jnp.int32)
    blocks = jnp.mod(device[:, None] * BR_DEV - 2 * BR_DEV + chosen, NB)
    return blocks.astype(jnp.int32)


def draw_counts(key, part):
    key = jax.random.fold_in(key, 7)
    raw_draw = jax.random.randint(key, (TYPES, TIME), 0, 16)
    return jnp.maximum(raw_draw - 12, 0).astype(jnp.int32)


def draw_decay_rate(key, part):
    basis_role = basis_roles(key)
    key = jax.random.fold_in(key, 11)
    unit_draw = jax.random.uniform(key, (BASES,), jnp.float32)
    rapid_rate = 0.02 * jnp.exp2(unit_draw)
    middle_rate = 0.005 * jnp.exp2(unit_draw)
    gentle_rate = 0.0001 * jnp.power(5.0, unit_draw)
    chosen_rate = jnp.where(basis_role < 2, rapid_rate, jnp.where(basis_role < 4, middle_rate, gentle_rate))
    return chosen_rate.astype(jnp.float32)


def draw_mixing(key, part):
    basis_role = basis_roles(key)
    key = jax.random.fold_in(key, 13)
    sign_key, spread_key, gentle_key = jax.random.split(key, 3)
    signs = jnp.where(jax.random.bernoulli(sign_key, 0.5, (1, TYPES)), 1.0, -1.0).astype(jnp.float32)
    spread = jax.random.uniform(spread_key, (BASES, TYPES), jnp.float32, 0.75, 1.25)
    gentle_weight = jnp.clip(jax.random.normal(gentle_key, (BASES, TYPES), jnp.float32), -4.0, 4.0)
    excite = 4.5 * signs * spread
    role_column = basis_role[:, None]
    chosen_weight = jnp.where(role_column < 2, excite, jnp.where(role_column < 4, -excite, gentle_weight))
    return chosen_weight.astype(jnp.float32)


def level_of(key, dims, pieces, low, largest):
    def one(axis_at, parts):
        steps = jax.random.uniform(jax.random.fold_in(jax.random.fold_in(key, 6), axis_at), (parts,), jnp.float32, low / len(pieces), largest / len(pieces))
        return jnp.repeat(jnp.exp(steps), dims[axis_at] // parts).reshape((-1,) + (1,) * (len(dims) - axis_at - 1))

    gain = one(*pieces[0])
    for cut in pieces[1:]:
        gain = gain * one(*cut)
    return gain


def normal_values(own_key, extent, width, limit, shards=(), held_as=jnp.bfloat16):
    drawn = width * jax.random.normal(own_key, extent, jnp.float32)
    if shards:
        drawn = drawn * level_of(own_key, extent, shards, -0.22, 0.18)
    return jnp.clip(drawn, -limit, limit).astype(held_as)


def setup_inputs(seed: int = 0) -> dict:
    key_of = jax.random.split(jax.random.key(seed), 7)
    counts = draw_counts(jax.random.fold_in(key_of[6], 71), 0)
    col_blocks = draw_col_blocks(jax.random.fold_in(key_of[6], 71), 0)
    kernel = normal_values(key_of[2], (NB, SLOTS, BLK, BLK), (SLOTS * BLK) ** -0.5, 0.109375, ((0, 8),))
    mixing = draw_mixing(jax.random.fold_in(key_of[6], 71), 0)
    decay_rate = draw_decay_rate(jax.random.fold_in(key_of[6], 71), 0)
    baseline = normal_values(key_of[5], (TYPES,), 1.0, 6.0, ((0, 8),), jnp.float32)
    return {"counts": counts, "col_blocks": col_blocks, "kernel": kernel, "mixing": mixing, "decay_rate": decay_rate, "baseline": baseline}


def reference(counts, col_blocks, kernel, mixing, decay_rate, baseline):
    amounts = counts.astype(jnp.float32)
    factor = jnp.exp(-decay_rate)
    weighted = mixing * decay_rate[:, None]

    def advance(states, column):
        driving_now = jnp.sum(weighted * states, axis=0)
        states_next = factor[:, None] * (states + column[None, :])
        return states_next, driving_now.astype(jnp.bfloat16)

    _, drives = lax.scan(advance, jnp.zeros((BASES, TYPES), jnp.float32), amounts.T)
    driving = drives.T.reshape(NB, BLK, TIME)

    def one_block_row(inputs):
        weights, indices = inputs
        blocks = jnp.take(driving, indices, axis=0).astype(jnp.float32)
        return jnp.einsum("kab,kbt->at", weights.astype(jnp.float32), blocks)

    potential = lax.map(one_block_row, (kernel, col_blocks)).reshape(TYPES, TIME)
    potential = potential + baseline[:, None]
    return jax.nn.softplus(potential).astype(jnp.bfloat16)
```

```python
import functools

import jax
import jax.numpy as jnp
from jax import lax
from jax.experimental import pallas as pl
from jax.experimental.pallas import tpu as pltpu
from jax.sharding import PartitionSpec as P

MESH = pl.DeviceIdType.MESH
F32 = jnp.float32
BF16 = jnp.bfloat16
LEN = 128
TILE = 256


def split(x):
    high = x.astype(BF16)
    return high, (x - high.astype(F32)).astype(BF16)


def body(
    n_rows, n_tm,
    decay_ref, cols_ref, counts_hbm, kernel_hbm, mixing_ref, baseline_ref, out_hbm,
    counts, amounts, blocks, dense, own, win, total, result, table, entry3, states, hist, leaving, columns,
    load_sem, out_sem, send_sem, recv_sem, pass_sem, hist_send, hist_recv,
):
    n_types, panel = counts.shape
    chunks = panel // LEN
    bases = mixing_ref.shape[0]
    n_blocks = blocks.shape[0] - 1
    brows, slots = cols_ref.shape
    width = n_types // brows
    row, col = lax.axis_index("rows"), lax.axis_index("tm")
    odd = lax.rem(row, 2)
    up, down = lax.rem(row + 2, n_rows), lax.rem(row + n_rows - 2, n_rows)
    mate = row + 1 - 2 * odd
    peers = [lax.rem(col + k, n_tm) for k in range(1, n_tm)]

    load_counts = pltpu.make_async_copy(counts_hbm, counts, load_sem.at[0])
    load_blocks = pltpu.make_async_copy(kernel_hbm, blocks.at[pl.ds(0, n_blocks)], load_sem.at[1])
    load_counts.start()
    load_blocks.start()

    barrier = pltpu.get_barrier_semaphore()
    for r in (up, down, mate):
        pl.semaphore_signal(barrier, inc=1, device_id=(r, col), device_id_type=MESH)
    for c in peers:
        pl.semaphore_signal(barrier, inc=1, device_id=(row, c), device_id_type=MESH)

    rates = [decay_ref[b] for b in range(bases)]
    basis_id = lax.broadcasted_iota(jnp.int32, (bases, LEN), 0)
    rate_tile = jnp.zeros((bases, LEN), F32)
    for b in range(bases):
        rate_tile = jnp.where(basis_id == b, rates[b], rate_tile)
    rate = rate_tile[:, 0:1]

    since = lax.broadcasted_iota(jnp.int32, (bases, panel), 1)
    exits = []
    for m in range(1, chunks + 1):
        gap = (LEN * m - since).astype(F32)
        exits.append(jnp.where(since < LEN * m, jnp.exp(-rate * jnp.maximum(gap, 0.0)), 0.0))
    exits_high, exits_low = split(jnp.concatenate(exits, axis=0))
    exit_table = jnp.concatenate([exits_high, exits_low], axis=0)

    load_counts.wait()
    amounts[...] = counts[...].astype(F32).astype(BF16)
    both = lax.dot_general(
        exit_table, amounts[...], (((1,), (1,)), ((), ())), preferred_element_type=F32
    )
    states[...] = both[: chunks * bases] + both[chunks * bases :]
    leaving[...] = states[(chunks - 1) * bases :, :]
    pl.semaphore_wait(barrier, 3 + n_tm - 1)

    hist_copies = []
    for k, c in enumerate(peers):
        copy = pltpu.make_async_remote_copy(
            src_ref=leaving, dst_ref=hist.at[col], send_sem=hist_send.at[k], recv_sem=hist_recv.at[col],
            device_id=(row, c), device_id_type=MESH,
        )
        copy.start()
        hist_copies.append(copy)

    distance = (
        lax.broadcasted_iota(jnp.int32, (LEN, LEN), 1) - lax.broadcasted_iota(jnp.int32, (LEN, LEN), 0)
    )
    lag = jnp.maximum(distance, 0).astype(F32)
    for b in range(bases):
        high, low = split(jnp.where(distance > 0, jnp.exp(-rates[b] * lag), 0.0))
        table[0:LEN, b * LEN : (b + 1) * LEN] = high
        table[LEN : 2 * LEN, b * LEN : (b + 1) * LEN] = low
    offset = lax.broadcasted_iota(jnp.int32, (bases, LEN), 1).astype(F32)
    entry_high, entry_low = split(jnp.exp(-rate_tile * offset))
    entry3[...] = jnp.concatenate([entry_high, entry_high, entry_low, entry_low], axis=0)
    weights = mixing_ref[...] * rate
    stacked = jnp.concatenate([weights, jnp.broadcast_to(baseline_ref[...], (bases, n_types))], axis=0)
    columns[...] = jnp.transpose(stacked)

    incoming = jnp.zeros((bases, n_types), F32)
    for k, c in enumerate(peers):
        pltpu.make_async_remote_copy(
            src_ref=leaving, dst_ref=hist.at[c], send_sem=hist_send.at[k], recv_sem=hist_recv.at[c],
            device_id=(row, c), device_id_type=MESH,
        ).wait_recv()
        panels = jnp.maximum(col - 1 - c, 0).astype(F32)
        factor = jnp.exp(-rate * (panels * panel)) * jnp.where(c < col, 1.0, 0.0)
        incoming = incoming + hist[c] * factor

    def send(slot_here, slot_there, m, target, sem):
        src = own.at[m] if slot_here is None else win.at[slot_here, m]
        return pltpu.make_async_remote_copy(
            src_ref=src, dst_ref=win.at[slot_there, m], send_sem=sem, recv_sem=recv_sem.at[slot_there, m],
            device_id=(target, col), device_id_type=MESH,
        )

    sends = []
    for m in range(chunks):
        state = incoming * jnp.exp(-rate * float(LEN * m))
        if m > 0:
            state = state + states[(m - 1) * bases : m * bases, :]
        state_high, state_low = split(weights * state)
        carried = jnp.concatenate([state_high, state_low, state_high, state_low], axis=0)
        for t in range(n_types // TILE):
            rows = slice(t * TILE, (t + 1) * TILE)
            piece = amounts[rows, m * LEN : (m + 1) * LEN]
            inside = jnp.dot(
                jnp.concatenate([piece, piece], axis=1), table[...], preferred_element_type=F32
            )
            drive = lax.dot_general(
                carried[:, rows], entry3[...], (((0,), (0,)), ((), ())), preferred_element_type=F32
            )
            for b in range(bases):
                drive = drive + columns[rows, b : b + 1] * inside[:, b * LEN : (b + 1) * LEN]
            own[m, rows, :] = drive.astype(BF16)
        for k, (there, target) in enumerate(((0, up), (4, down), (1 + 2 * odd, mate))):
            copy = send(None, there, m, target, send_sem.at[k, m])
            copy.start()
            sends.append(copy)

    load_blocks.wait()
    blocks[n_blocks] = jnp.zeros(blocks.shape[1:], BF16)

    def place(step, carry):
        d, rest = step // (brows * brows), lax.rem(step, brows * brows)
        i, q = rest // brows, lax.rem(rest, brows)
        wanted = lax.rem(row + n_rows + d - 2, n_rows) * brows + q
        at = n_blocks
        for s in range(slots):
            at = jnp.where(cols_ref[i, s] == wanted, i * slots + s, at)
        dense[d, pl.ds(pl.multiple_of(i * width, width), width), pl.ds(pl.multiple_of(q * width, width), width)] = (
            blocks[at]
        )
        return carry

    lax.fori_loop(0, 5 * brows * brows, place, 0)

    def multiply(d, m, source, first=False, last=False):
        for t in range(n_types // TILE):
            rows = slice(t * TILE, (t + 1) * TILE)
            part = jnp.dot(dense[d, rows, :], source, preferred_element_type=F32)
            if first:
                part = part + columns[rows, bases : bases + 1]
            else:
                part = part + total[m, rows, :]
            if last:
                part = jnp.maximum(part, 0.0) + jnp.log1p(jnp.exp(-jnp.abs(part)))
                result[m, rows, :] = part.astype(BF16)
            else:
                total[m, rows, :] = part

    def arrived(slot, m):
        send(None, slot, m, mate, send_sem.at[0, m]).wait_recv()

    far, near = 4 - 4 * odd, 4 * odd
    mate_slot, passed_slot = 3 - 2 * odd, 1 + 2 * odd
    outs = []

    def finish(m):
        arrived(passed_slot, m)
        multiply(passed_slot, m, win[passed_slot, m], last=True)
        out = pltpu.make_async_copy(result.at[m], out_hbm.at[:, pl.ds(m * LEN, LEN)], out_sem.at[m])
        out.start()
        outs.append(out)

    for m in range(chunks):
        multiply(2, m, own[m], first=True)
    for m in range(chunks):
        arrived(far, m)
        copy = send(far, 3 - 2 * odd, m, mate, pass_sem.at[m])
        copy.start()
        sends.append(copy)
        multiply(far, m, win[far, m])
        arrived(mate_slot, m)
        multiply(mate_slot, m, win[mate_slot, m])
        if m > 0:
            finish(m - 1)
        arrived(near, m)
        multiply(near, m, win[near, m])
    finish(chunks - 1)
    for copy in sends + hist_copies:
        copy.wait_send()
    for out in outs:
        out.wait()


def local(n_rows, n_tm, counts, col_blocks, kernel, mixing, decay_rate, baseline):
    n_types, panel = counts.shape
    chunks = panel // LEN
    brows, slots, width, _ = kernel.shape
    bases = decay_rate.shape[0]
    vmem, smem, hbm = pltpu.VMEM, pltpu.SMEM, pl.ANY
    dma = pltpu.SemaphoreType.DMA
    return pl.pallas_call(
        functools.partial(body, n_rows, n_tm),
        out_shape=jax.ShapeDtypeStruct((n_types, panel), BF16),
        in_specs=[
            pl.BlockSpec(memory_space=smem),
            pl.BlockSpec(memory_space=smem),
            pl.BlockSpec(memory_space=hbm),
            pl.BlockSpec(memory_space=hbm),
            pl.BlockSpec(memory_space=vmem),
            pl.BlockSpec(memory_space=vmem),
        ],
        out_specs=pl.BlockSpec(memory_space=hbm),
        scratch_shapes=[
            vmem((n_types, panel), jnp.int32),
            vmem((n_types, panel), BF16),
            vmem((brows * slots + 1, width, width), BF16),
            vmem((5, n_types, n_types), BF16),
            vmem((chunks, n_types, LEN), BF16),
            vmem((5, chunks, n_types, LEN), BF16),
            vmem((chunks, n_types, LEN), F32),
            vmem((chunks, n_types, LEN), BF16),
            vmem((2 * LEN, bases * LEN), BF16),
            vmem((4 * bases, LEN), BF16),
            vmem((chunks * bases, n_types), F32),
            vmem((n_tm, bases, n_types), F32),
            vmem((bases, n_types), F32),
            vmem((n_types, 2 * bases), F32),
            dma((2,)),
            dma((chunks,)),
            dma((3, chunks)),
            dma((5, chunks)),
            dma((chunks,)),
            dma((n_tm,)),
            dma((n_tm,)),
        ],
        compiler_params=pltpu.CompilerParams(
            collective_id=0, has_side_effects=True, vmem_limit_bytes=56 * 1024 * 1024
        ),
        cost_estimate=pl.CostEstimate(
            flops=2 * n_types * 5 * n_types * panel, bytes_accessed=12 * 1024 * 1024, transcendentals=0
        ),
    )(decay_rate, col_blocks, counts, kernel.reshape(brows * slots, width, width), mixing, baseline.reshape(1, n_types))


def solution(mesh):
    in_specs = (
        P("rows", "tm"),
        P("rows", None),
        P("rows", None, None, None),
        P(None, "rows"),
        P(),
        P("rows"),
    )
    return jax.shard_map(
        functools.partial(local, mesh.shape["rows"], mesh.shape["tm"]),
        mesh=mesh, in_specs=in_specs, out_specs=P("rows", "tm"), check_vma=False,
    )
```

```python
import functools

import jax
import jax.numpy as jnp
from jax import lax
from jax.experimental import pallas as pl
from jax.experimental.pallas import tpu as pltpu
from jax.sharding import PartitionSpec as P

MESH = pl.DeviceIdType.MESH
F32 = jnp.float32
BF16 = jnp.bfloat16
LEN = 128
TILE = 256


def split(x):
    high = x.astype(BF16)
    return high, (x - high.astype(F32)).astype(BF16)


def body(
    n_rows, n_tm,
    decay_ref, cols_ref, counts_hbm, kernel_hbm, mixing_hbm, baseline_hbm, out_hbm,
    mixing_ref, baseline_ref, counts, amounts, blocks, dense, own, win, total, result, table, entry3, states, hist, leaving, columns,
    load_sem, out_sem, send_sem, recv_sem, pass_sem, hist_send, hist_recv,
):
    n_types, panel = counts.shape
    chunks = panel // LEN
    bases = mixing_ref.shape[0]
    n_blocks = blocks.shape[0] - 1
    brows, slots = cols_ref.shape
    width = n_types // brows
    row, col = lax.axis_index("rows"), lax.axis_index("tm")
    odd = lax.rem(row, 2)
    up, down = lax.rem(row + 2, n_rows), lax.rem(row + n_rows - 2, n_rows)
    mate = row + 1 - 2 * odd
    peers = [lax.rem(col + k, n_tm) for k in range(1, n_tm)]

    load_counts = pltpu.make_async_copy(counts_hbm, counts, load_sem.at[0])
    load_blocks = pltpu.make_async_copy(kernel_hbm, blocks.at[pl.ds(0, n_blocks)], load_sem.at[1])
    load_mixing = pltpu.make_async_copy(mixing_hbm, mixing_ref, load_sem.at[2])
    load_baseline = pltpu.make_async_copy(baseline_hbm, baseline_ref, load_sem.at[3])
    load_counts.start()
    load_mixing.start()
    load_baseline.start()
    load_blocks.start()

    barrier = pltpu.get_barrier_semaphore()
    for r in (up, down, mate):
        pl.semaphore_signal(barrier, inc=1, device_id=(r, col), device_id_type=MESH)
    for c in peers:
        pl.semaphore_signal(barrier, inc=1, device_id=(row, c), device_id_type=MESH)

    rates = [decay_ref[b] for b in range(bases)]
    basis_id = lax.broadcasted_iota(jnp.int32, (bases, LEN), 0)
    rate_tile = jnp.zeros((bases, LEN), F32)
    for b in range(bases):
        rate_tile = jnp.where(basis_id == b, rates[b], rate_tile)
    rate = rate_tile[:, 0:1]

    since = lax.broadcasted_iota(jnp.int32, (bases, panel), 1)
    exits = []
    for m in range(1, chunks + 1):
        gap = (LEN * m - since).astype(F32)
        exits.append(jnp.where(since < LEN * m, jnp.exp(-rate * jnp.maximum(gap, 0.0)), 0.0))
    exits_high, exits_low = split(jnp.concatenate(exits, axis=0))
    exit_table = jnp.concatenate([exits_high, exits_low], axis=0)

    distance = (
        lax.broadcasted_iota(jnp.int32, (LEN, LEN), 1) - lax.broadcasted_iota(jnp.int32, (LEN, LEN), 0)
    )
    lag = jnp.maximum(distance, 0).astype(F32)
    for b in range(bases):
        high, low = split(jnp.where(distance > 0, jnp.exp(-rates[b] * lag), 0.0))
        table[0:LEN, b * LEN : (b + 1) * LEN] = high
        table[LEN : 2 * LEN, b * LEN : (b + 1) * LEN] = low
    offset = lax.broadcasted_iota(jnp.int32, (bases, LEN), 1).astype(F32)
    entry_high, entry_low = split(jnp.exp(-rate_tile * offset))
    entry3[...] = jnp.concatenate([entry_high, entry_high, entry_low, entry_low], axis=0)
    load_counts.wait()
    amounts[...] = counts[...].astype(F32).astype(BF16)
    both = lax.dot_general(
        exit_table, amounts[...], (((1,), (1,)), ((), ())), preferred_element_type=F32
    )
    states[...] = both[: chunks * bases] + both[chunks * bases :]
    leaving[...] = states[(chunks - 1) * bases :, :]
    pl.semaphore_wait(barrier, 3 + n_tm - 1)

    hist_copies = []
    for k, c in enumerate(peers):
        copy = pltpu.make_async_remote_copy(
            src_ref=leaving, dst_ref=hist.at[col], send_sem=hist_send.at[k], recv_sem=hist_recv.at[col],
            device_id=(row, c), device_id_type=MESH,
        )
        copy.start()
        hist_copies.append(copy)

    load_mixing.wait()
    load_baseline.wait()
    weights = mixing_ref[...] * rate
    stacked = jnp.concatenate([weights, jnp.broadcast_to(baseline_ref[...], (bases, n_types))], axis=0)
    columns[...] = jnp.transpose(stacked)


    def inside_part(m, t):
        piece = amounts[t * TILE : (t + 1) * TILE, m * LEN : (m + 1) * LEN]
        inside = jnp.dot(
            jnp.concatenate([piece, piece], axis=1), table[...], preferred_element_type=F32
        )
        drive = columns[t * TILE : (t + 1) * TILE, 0:1] * inside[:, 0:LEN]
        for b in range(1, bases):
            drive = drive + columns[t * TILE : (t + 1) * TILE, b : b + 1] * inside[:, b * LEN : (b + 1) * LEN]
        return drive

    tiles = n_types // TILE
    for t in range(tiles):
        total[0, t * TILE : (t + 1) * TILE, :] = inside_part(0, t)

    incoming = jnp.zeros((bases, n_types), F32)
    for k, c in enumerate(peers):
        pltpu.make_async_remote_copy(
            src_ref=leaving, dst_ref=hist.at[c], send_sem=hist_send.at[k], recv_sem=hist_recv.at[c],
            device_id=(row, c), device_id_type=MESH,
        ).wait_recv()
        panels = jnp.maximum(col - 1 - c, 0).astype(F32)
        factor = jnp.exp(-rate * (panels * panel)) * jnp.where(c < col, 1.0, 0.0)
        incoming = incoming + hist[c] * factor

    def send(slot_here, slot_there, m, t, target, sem):
        part = pl.ds(t * TILE, TILE)
        src = own.at[m, part] if slot_here is None else win.at[slot_here, m, part]
        return pltpu.make_async_remote_copy(
            src_ref=src, dst_ref=win.at[slot_there, m, part], send_sem=sem,
            recv_sem=recv_sem.at[slot_there, m, t], device_id=(target, col), device_id_type=MESH,
        )

    sends = []
    first_target = jnp.where(odd == 1, up, down)
    second_target = jnp.where(odd == 1, down, up)
    routes = ((4 - 4 * odd, first_target), (1 + 2 * odd, mate))

    def send_near(m):
        for t in range(tiles):
            copy = send(None, 4 * odd, m, t, second_target, send_sem.at[2, m, t])
            copy.start()
            sends.append(copy)

    for m in range(chunks):
        state = incoming * jnp.exp(-rate * float(LEN * m))
        if m > 0:
            state = state + states[(m - 1) * bases : m * bases, :]
        state_high, state_low = split(weights * state)
        carried = jnp.concatenate([state_high, state_low, state_high, state_low], axis=0)
        for t in range(tiles):
            rows = slice(t * TILE, (t + 1) * TILE)
            inside = total[0, rows, :] if m == 0 else inside_part(m, t)
            drive = inside + lax.dot_general(
                carried[:, rows], entry3[...], (((0,), (0,)), ((), ())), preferred_element_type=F32
            )
            own[m, rows, :] = drive.astype(BF16)
            for k, (there, target) in enumerate(routes):
                copy = send(None, there, m, t, target, send_sem.at[k, m, t])
                copy.start()
                sends.append(copy)

    for n in range(chunks // 2):
        send_near(n)
    load_blocks.wait()
    blocks[n_blocks] = jnp.zeros(blocks.shape[1:], BF16)

    def place(step, carry):
        d, rest = step // (brows * brows), lax.rem(step, brows * brows)
        i, q = rest // brows, lax.rem(rest, brows)
        wanted = lax.rem(row + n_rows + d - 2, n_rows) * brows + q
        at = n_blocks
        for s in range(slots):
            at = jnp.where(cols_ref[i, s] == wanted, i * slots + s, at)
        dense[d, pl.ds(pl.multiple_of(i * width, width), width), pl.ds(pl.multiple_of(q * width, width), width)] = (
            blocks[at]
        )
        return carry

    lax.fori_loop(0, 5 * brows * brows, place, 0)

    def multiply(d, m, source, first=False, last=False):
        for t in range(n_types // TILE):
            rows = slice(t * TILE, (t + 1) * TILE)
            part = jnp.dot(dense[d, rows, :], source, preferred_element_type=F32)
            if first:
                part = part + columns[rows, bases : bases + 1]
            else:
                part = part + total[m, rows, :]
            if last:
                part = jnp.maximum(part, 0.0) + jnp.log1p(jnp.exp(-jnp.abs(part)))
                result[m, rows, :] = part.astype(BF16)
            else:
                total[m, rows, :] = part

    def piece_arrived(slot, m, t):
        send(None, slot, m, t, mate, send_sem.at[0, m, t]).wait_recv()

    def arrived(slot, m):
        for t in range(tiles):
            piece_arrived(slot, m, t)

    far, near = 4 - 4 * odd, 4 * odd
    mate_slot, passed_slot = 3 - 2 * odd, 1 + 2 * odd
    outs = []

    def use(slot, m, last=False):
        arrived(slot, m)
        multiply(slot, m, win[slot, m], last=last)

    def finish(m):
        use(near, m, last=True)
        out = pltpu.make_async_copy(result.at[m], out_hbm.at[:, pl.ds(m * LEN, LEN)], out_sem.at[m])
        out.start()
        outs.append(out)

    for n in range(chunks // 2, chunks):
        send_near(n)
    for m in range(chunks):
        for t in range(tiles):
            piece_arrived(far, m, t)
            copy = send(far, 3 - 2 * odd, m, t, mate, pass_sem.at[m, t])
            copy.start()
            sends.append(copy)
            if t == 0:
                multiply(2, m, own[m], first=True)
        multiply(far, m, win[far, m])
    for m in range(chunks):
        use(mate_slot, m)
    for m in range(chunks):
        use(passed_slot, m)
        finish(m)
    for copy in sends + hist_copies:
        copy.wait_send()
    for out in outs:
        out.wait()


def local(n_rows, n_tm, counts, col_blocks, kernel, mixing, decay_rate, baseline):
    n_types, panel = counts.shape
    chunks = panel // LEN
    brows, slots, width, _ = kernel.shape
    bases = decay_rate.shape[0]
    vmem, smem, hbm = pltpu.VMEM, pltpu.SMEM, pl.ANY
    dma = pltpu.SemaphoreType.DMA
    return pl.pallas_call(
        functools.partial(body, n_rows, n_tm),
        out_shape=jax.ShapeDtypeStruct((n_types, panel), BF16),
        in_specs=[
            pl.BlockSpec(memory_space=smem),
            pl.BlockSpec(memory_space=smem),
            pl.BlockSpec(memory_space=pltpu.HBM),
            pl.BlockSpec(memory_space=pltpu.HBM),
            pl.BlockSpec(memory_space=pltpu.HBM),
            pl.BlockSpec(memory_space=pltpu.HBM),
        ],
        out_specs=pl.BlockSpec(memory_space=hbm),
        scratch_shapes=[
            vmem((bases, n_types), F32),
            vmem((1, n_types), F32),
            vmem((n_types, panel), jnp.int32),
            vmem((n_types, panel), BF16),
            vmem((brows * slots + 1, width, width), BF16),
            vmem((5, n_types, n_types), BF16),
            vmem((chunks, n_types, LEN), BF16),
            vmem((5, chunks, n_types, LEN), BF16),
            vmem((chunks, n_types, LEN), F32),
            vmem((chunks, n_types, LEN), BF16),
            vmem((2 * LEN, bases * LEN), BF16),
            vmem((4 * bases, LEN), BF16),
            vmem((chunks * bases, n_types), F32),
            vmem((n_tm, bases, n_types), F32),
            vmem((bases, n_types), F32),
            vmem((n_types, 2 * bases), F32),
            dma((4,)),
            dma((chunks,)),
            dma((3, chunks, n_types // TILE)),
            dma((5, chunks, n_types // TILE)),
            dma((chunks, n_types // TILE)),
            dma((n_tm,)),
            dma((n_tm,)),
        ],
        compiler_params=pltpu.CompilerParams(
            collective_id=0, has_side_effects=True, vmem_limit_bytes=56 * 1024 * 1024
        ),
        cost_estimate=pl.CostEstimate(
            flops=2 * n_types * 5 * n_types * panel, bytes_accessed=12 * 1024 * 1024, transcendentals=0
        ),
    )(decay_rate, col_blocks, counts, kernel.reshape(brows * slots, width, width), mixing, baseline.reshape(1, n_types))


def solution(mesh):
    in_specs = (
        P("rows", "tm"),
        P("rows", None),
        P("rows", None, None, None),
        P(None, "rows"),
        P(),
        P("rows"),
    )
    return jax.shard_map(
        functools.partial(local, mesh.shape["rows"], mesh.shape["tm"]),
        mesh=mesh, in_specs=in_specs, out_specs=P("rows", "tm"), check_vma=False,
    )
```
